32 devices in a mesh: row: 8 (over z, x), col: 4 (over y, core).
Axes of the slice: x: 2, y: 2, z: 4, core: 2. Of those that a mesh axis runs over, the one named last changes fastest.
Arguments:
- tiles: bfloat16 [8, 4, 64, 128, 128], P('row', 'col'), may hold values from -0.078125 to 0.078125
- positions: int32 [8, 4, 64], replicated, may hold values from 0 to 15, as said below
- demand: bfloat16 [16384, 128], P(('row', 'col')), may hold values from -6 to 6
- value_added: bfloat16 [16384, 128], P(('row', 'col')), may hold values from -6 to 6
- extracted: int32 [128], replicated, may hold values from 0 to 127
Outputs:
- quantity: float32 [16384, 128], P(('row', 'col'))
- price: float32 [16384, 128], P(('row', 'col'))
The draws below stay inside these ranges and needn't reach their ends.
Inputs may be any that keep to these rules, and one draw needn't show every extreme that they name: Within each device's slots d * 2 to d * 2 + 1 the 2 positions differ.
All inputs are finite; a program needn't handle non-finite values.
Results may differ from the reference program's by a relative error of at most 0.0011.
Values may be sent and summed in bfloat16 or wider, within the bound.
A program may use at most 192 MiB of HBM per device.

```python
import jax
import jax.numpy as jnp
from jax import lax

TB = 128
RB = 16
S = 128
CAP = 2
TERMS = 3
GROUPS = 128
NB = 128
N = 16384
SLOTS = 64
N_ROW = 8
N_COL = 4


def draw_positions(key, part):
    quarter = RB // N_COL
    patch_size = quarter * quarter
    targets = N_ROW * N_COL
    scores = jax.random.randint(key, (N_ROW, N_COL, targets, patch_size), 0, 1048576)
    scores = scores * patch_size + jnp.arange(patch_size, dtype=jnp.int32)
    ranking = jnp.argsort(scores, axis=-1)
    return ranking[..., :CAP].astype(jnp.int32).reshape(N_ROW, N_COL, targets * CAP)


def plant(array, stream_key, least, top_value):
    shape = array.shape
    spot = [jax.random.randint(jax.random.fold_in(stream_key, axis), (), 0, shape[axis]) for axis in range(len(shape))]
    array = array.at[tuple(spot)].set(least)
    longest = shape.index(max(shape))
    spot[longest] = (spot[longest] + 1) % shape[longest]
    return array.at[tuple(spot)].set(top_value)


def levels(key, dims, pieces, smallest, high):
    level = 1.0
    for position, blocks in pieces:
        steps = jax.random.uniform(jax.random.fold_in(jax.random.fold_in(key, 6), position), (blocks,), jnp.float32, smallest / len(pieces), high / len(pieces))
        level = level * jnp.repeat(jnp.exp(steps), dims[position] // blocks).reshape((-1,) + (1,) * (len(dims) - 1 - position))
    return level


def noise(key, extent, scale, bound, split=(), kind=jnp.bfloat16):
    gain = levels(key, extent, split, -0.22, 0.18) if split else 1.0
    entries = jax.random.normal(key, extent, jnp.float32) * scale * gain
    return jnp.minimum(jnp.maximum(entries, -bound), bound).astype(kind)


def setup_inputs(seed: int = 0) -> dict:
    seeds = jax.random.split(jax.random.key(seed), 6)
    return {
        "tiles": noise(seeds[0], (N_ROW, N_COL, SLOTS, TB, TB), (3 * TB * CAP * N_ROW * N_COL * N_COL // RB) ** -0.5, 0.078125, ((0, 8), (1, 4))),
        "positions": draw_positions(jax.random.fold_in(seeds[5], 71), 0),
        "demand": noise(seeds[2], (N, S), 1.0, 6.0, ((0, 32),)),
        "value_added": noise(seeds[3], (N, S), 1.0, 6.0, ((0, 32),)),
        "extracted": plant(jax.random.randint(seeds[4], (S,), 0, GROUPS), jax.random.fold_in(seeds[4], 1), 0, GROUPS - 1).astype(jnp.int32),
    }


def coordinates(positions):
    quarter = RB // N_COL
    source_row = jnp.arange(N_ROW, dtype=jnp.int32)[:, None, None]
    source_column = jnp.arange(N_COL, dtype=jnp.int32)[None, :, None]
    target = (jnp.arange(SLOTS, dtype=jnp.int32) // CAP)[None, None, :]
    block_row = source_row * RB + (target % N_COL) * quarter + positions // quarter
    block_column = (target // N_COL) * RB + source_column * quarter + positions % quarter
    return block_row.reshape(-1, SLOTS), block_column.reshape(-1, SLOTS)


def multiply(tiles, rows_at, columns_at, vector, transpose):
    flat = tiles.reshape(-1, SLOTS, TB, TB)

    def visit(total, item):
        tile_set, rows_here, columns_here = item
        tile_set = tile_set.astype(jnp.float32)
        if transpose:
            picked = vector[rows_here].astype(jnp.float32)
            products = jnp.einsum("nkt,nks->nts", tile_set, picked)
            return total.at[columns_here].add(products), None
        picked = vector[columns_here].astype(jnp.float32)
        products = jnp.einsum("ntk,nks->nts", tile_set, picked)
        return total.at[rows_here].add(products), None

    start = jnp.zeros((NB, TB, S), jnp.float32)
    return lax.scan(visit, start, (flat, rows_at, columns_at))[0]


def reference(tiles, positions, demand, value_added, extracted):
    keep_mask = (jnp.arange(NB, dtype=jnp.int32)[:, None] % GROUPS != extracted[None, :]).astype(jnp.float32)[:, None, :]
    rows_at, columns_at = coordinates(positions)

    def series(source, transpose):
        total = keep_mask * source.reshape(NB, TB, S).astype(jnp.float32)
        vector = total.astype(jnp.bfloat16)
        for term_number in range(TERMS):
            image = multiply(tiles, rows_at, columns_at, vector, transpose)
            masked = keep_mask * image
            total = total + masked
            vector = masked.astype(jnp.bfloat16)
        return total.reshape(NB * TB, S)

    return series(demand, False), series(value_added, True)
```

```python
import functools

import jax
import jax.numpy as jnp
from jax import lax
from jax.experimental import pallas as pl
from jax.experimental.pallas import tpu as pltpu
from jax.sharding import PartitionSpec as P

TERMS = 3
GROUPS = 128
LEVEL = 32000.0
MESH = pl.DeviceIdType.MESH


def pack(values, slot):
    rows = values.shape[0]
    top = jnp.max(jnp.abs(values), axis=0, keepdims=True)
    power = jnp.ceil(jnp.log2(jnp.maximum(top, 1e-30)))
    scaled = jnp.floor(values * (jnp.exp2(-power) * LEVEL) + 0.5)
    slot[pl.ds(0, rows), :] = scaled.astype(jnp.int32).astype(jnp.int16)
    slot[pl.ds(rows, 16), :] = (
        jnp.broadcast_to(power, (16, power.shape[1])).astype(jnp.int32).astype(jnp.int16)
    )


def unpack(slot, rows):
    power = slot[pl.ds(rows, 16), :].astype(jnp.int32).astype(jnp.float32)[0:1, :]
    values = slot[pl.ds(0, rows), :].astype(jnp.int32).astype(jnp.float32)
    return values * (jnp.exp2(power) * (1.0 / LEVEL))


def kernel(
    rows, columns, capacity, quarter, places, tiles, demand, value_added, gone, gone_down,
    quantity, price_out,
    stack, wide, gath_q, gath_p, here_q, here_p, spread_q, spread_p, price, total,
    send_x, send_z, send_q, got_x, got_z, got_q,
    tile_sem, out_sem, aqz_s, aqz_r, aqx_s, aqx_r, ap_s, ap_r, px_s, px_r, pz_s, pz_r, q_s, q_r,
):
    size = tiles.shape[1]
    scenarios = demand.shape[1]
    length = quarter * size
    slabs = rows // 2
    group = columns * capacity
    row, column = lax.axis_index("row"), lax.axis_index("col")
    slab, side = row // 2, row % 2
    partner = (slab * 2 + 1 - side, column)

    def slab_peer(step):
        return lax.rem(slab + step, slabs)

    def column_peer(step):
        return lax.rem(column + step, columns)

    def remote(src, dst, send, recv, device):
        return pltpu.make_async_remote_copy(
            src_ref=src, dst_ref=dst, send_sem=send, recv_sem=recv,
            device_id=device, device_id_type=MESH,
        )

    whole = pltpu.make_async_copy(tiles, stack, tile_sem.at[0])
    whole.start()

    def side_by_side(m):
        d, u = m // capacity, m % capacity
        place = pl.multiple_of(((d // columns) * capacity + u) * size, size)
        return pltpu.make_async_copy(
            tiles.at[m], wide.at[d % columns, :, pl.ds(place, size)], out_sem.at[m]
        )

    lax.fori_loop(0, rows * group, lambda m, _: (side_by_side(m).start(), 0)[1], 0)

    barrier = pltpu.get_barrier_semaphore()
    pl.semaphore_signal(barrier, inc=1, device_id=partner, device_id_type=MESH)
    for step in range(1, slabs):
        pl.semaphore_signal(
            barrier, inc=1, device_id=(slab_peer(step) * 2 + side, column), device_id_type=MESH
        )
    for step in range(1, columns):
        pl.semaphore_signal(
            barrier, inc=1, device_id=(row, column_peer(step)), device_id_type=MESH
        )

    first = (row * columns + column) * quarter
    for q in range(quarter):
        part = pl.ds(q * size, size)
        block = (first + q) % GROUPS
        keep = jnp.where(gone[...] != block, 1.0, 0.0)
        start = keep * demand[part, :].astype(jnp.float32)
        quantity[part, :] = start
        gath_q[0, row, part, :] = start.astype(jnp.bfloat16)
        keep_down = jnp.where(gone_down[...] != block, 1.0, 0.0)
        start = keep_down * value_added[part, :].astype(jnp.float32).T
        price[pl.ds(q * scenarios, scenarios), :] = start
        gath_p[0, column, pl.ds(q * scenarios, scenarios), :] = start.astype(jnp.bfloat16)

    pl.semaphore_wait(barrier, slabs + columns - 1)
    whole.wait()
    lax.fori_loop(0, rows * group, lambda m, _: (side_by_side(m).wait(), 0)[1], 0)

    def weight(ok):
        return jnp.full((16, 128), jnp.where(ok, 1.0, 0.0), jnp.float32).astype(jnp.bfloat16)

    def charge_part(t, owner):
        def fill(k, _):
            place = places[0, owner * group + k]
            at = (k // capacity) * quarter + place // quarter
            block = here_p[at // quarter, pl.ds((at % quarter) * scenarios, scenarios), :]
            block = block.reshape(scenarios // 16, 16, size)
            for q in range(quarter):
                spread_p[k, pl.ds(q * scenarios, scenarios), :] = (
                    block * weight(place % quarter == q)[None]
                ).reshape(scenarios, size)
            return 0

        lax.fori_loop(0, group, fill, 0, unroll=True)
        left = jnp.concatenate([spread_p[k] for k in range(group)], axis=1)
        right = stack[pl.ds(owner * group, group)].reshape(group * size, size)
        return jnp.dot(left, right, preferred_element_type=jnp.float32)

    def supply_part(t, owner):
        width = 4

        def chunk(j, _):
            for k in range(width * capacity):
                source = j * width + k // capacity
                place = places[0, (source * columns + owner) * capacity + k % capacity]
                block = here_q[source, pl.ds((place % quarter) * size, size), :]
                block = block.reshape(size // 16, 16, scenarios)
                for q in range(quarter):
                    spread_q[pl.ds(k * size, size), pl.ds(q * scenarios, scenarios)] = (
                        block * weight(place // quarter == q)[None]
                    ).reshape(size, scenarios)
            depth = width * capacity * size
            left = wide[owner, :, pl.ds(pl.multiple_of(j * depth, depth), depth)]
            product = jnp.dot(left, spread_q[...], preferred_element_type=jnp.float32)
            for q in range(quarter):
                part = product[:, q * scenarios : (q + 1) * scenarios]
                total[pl.ds(q * size, size), :] += part
            return 0

        total[...] = jnp.zeros_like(total)
        lax.fori_loop(0, rows // width, chunk, 0)

    def term(t, _):
        def own_over(step):
            return remote(
                gath_q.at[t, row], gath_q.at[t, row], aqz_s.at[t, step], aqz_r.at[t, slab],
                (slab_peer(step) * 2 + side, column),
            )

        def from_over(z):
            at = z * 2 + side
            return remote(
                gath_q.at[t, at], gath_q.at[t, at], aqz_s.at[t, 0], aqz_r.at[t, z], partner
            )

        def across(z):
            at = z * 2 + side
            return remote(
                gath_q.at[t, at], gath_q.at[t, at], aqx_s.at[t, z], aqx_r.at[t, z], partner
            )

        def from_across(z):
            at = z * 2 + 1 - side
            return remote(
                gath_q.at[t, at], gath_q.at[t, at], aqx_s.at[t, z], aqx_r.at[t, z], partner
            )

        def charge_to(step):
            return remote(
                gath_p.at[t, column], gath_p.at[t, column], ap_s.at[t, step],
                ap_r.at[t, column], (row, column_peer(step)),
            )

        def charge_from(c):
            return remote(
                gath_p.at[t, c], gath_p.at[t, c], ap_s.at[t, 0], ap_r.at[t, c], partner
            )

        def cost_across(z):
            return remote(
                send_x.at[z], got_x.at[t, z], px_s.at[t, z], px_r.at[t, z], partner
            )

        def cost_over(step):
            return remote(
                send_z.at[step], got_z.at[t, slab], pz_s.at[t, step], pz_r.at[t, slab],
                (slab_peer(step) * 2 + side, column),
            )

        def cost_from(z):
            return remote(
                send_z.at[0], got_z.at[t, z], pz_s.at[t, 0], pz_r.at[t, z], partner
            )

        def image_to(step):
            return remote(
                send_q.at[step], got_q.at[t, column], q_s.at[t, step], q_r.at[t, column],
                (row, column_peer(step)),
            )

        def image_from(c):
            return remote(
                send_q.at[0], got_q.at[t, c], q_s.at[t, 0], q_r.at[t, c], partner
            )

        def each(low, high, body):
            lax.fori_loop(low, high, lambda i, _: (body(i), 0)[1], 0)

        each(1, columns, lambda s: charge_to(s).start())
        each(1, slabs, lambda s: own_over(s).start())
        across(slab).start()

        each(1, columns, lambda s: charge_from(column_peer(s)).wait_recv())
        here_p[...] = gath_p[t]

        def give_across(s):
            z = slab_peer(s)
            pack(charge_part(t, z * 2 + 1 - side), send_x.at[z])
            cost_across(z).start()

        each(1, slabs + 1, give_across)

        def forward(s):
            z = slab_peer(s)
            from_over(z).wait_recv()
            across(z).start()

        each(1, slabs, forward)

        def give_over(s):
            z = slab_peer(s)
            mine = charge_part(t, z * 2 + side)
            cost_across(z).wait_recv()
            pack(mine + unpack(got_x.at[t, z], length), send_z.at[s])
            cost_over(s).start()

        each(1, slabs, give_over)

        each(0, slabs, lambda z: from_across(z).wait_recv())

        def bring(i):
            here_q[i] = gath_q[t, i]

        each(0, rows, bring)

        def give_image(s):
            supply_part(t, column_peer(s))
            pack(total[...], send_q.at[s])
            image_to(s).start()

        each(1, columns, give_image)
        supply_part(t, column)
        image = total[...]
        for s in range(1, columns):
            c = column_peer(s)
            image_from(c).wait_recv()
            image += unpack(got_q.at[t, c], length)
        for q in range(quarter):
            part = pl.ds(q * size, size)
            keep = jnp.where(gone[...] != (first + q) % GROUPS, 1.0, 0.0)
            masked = keep * image[q * size : (q + 1) * size]
            quantity[part, :] += masked
            gath_q[lax.rem(t + 1, TERMS), row, part, :] = masked.astype(jnp.bfloat16)

        mine = charge_part(t, row)
        cost_across(slab).wait_recv()
        total[...] = mine + unpack(got_x.at[t, slab], length)

        def take_over(s):
            z = slab_peer(s)
            cost_from(z).wait_recv()
            total[...] += unpack(got_z.at[t, z], length)

        each(1, slabs, take_over)
        for q in range(quarter):
            part = pl.ds(q * scenarios, scenarios)
            keep_down = jnp.where(gone_down[...] != (first + q) % GROUPS, 1.0, 0.0)
            masked = keep_down * total[part, :]
            price[part, :] += masked
            gath_p[lax.rem(t + 1, TERMS), column, part, :] = masked.astype(jnp.bfloat16)

        each(1, columns, lambda s: charge_to(s).wait_send())
        each(1, slabs, lambda s: own_over(s).wait_send())
        each(0, slabs, lambda z: across(z).wait_send())
        each(0, slabs, lambda z: cost_across(z).wait_send())
        each(1, slabs, lambda s: cost_over(s).wait_send())
        each(1, columns, lambda s: image_to(s).wait_send())
        return 0

    lax.fori_loop(0, TERMS, term, 0)
    for q in range(quarter):
        price_out[pl.ds(q * size, size), :] = price[pl.ds(q * scenarios, scenarios), :].T


def shards(tiles, positions, demand, value_added, extracted):
    rows, columns = lax.axis_size("row"), lax.axis_size("col")
    slots, size = tiles.shape[2], tiles.shape[-1]
    length, scenarios = demand.shape
    quarter = length // size
    capacity = slots // (rows * columns)
    slabs = rows // 2
    places = lax.dynamic_slice(
        positions, (lax.axis_index("row"), lax.axis_index("col"), 0), (1, 1, slots)
    ).reshape(1, slots)
    dma = pltpu.SemaphoreType.DMA
    vmem = pl.BlockSpec(memory_space=pltpu.VMEM)
    bf16, f32, i16 = jnp.bfloat16, jnp.float32, jnp.int16
    packed = (length + 16, scenarios)
    return pl.pallas_call(
        functools.partial(kernel, rows, columns, capacity, quarter),
        out_shape=(
            jax.ShapeDtypeStruct((length, scenarios), f32),
            jax.ShapeDtypeStruct((length, scenarios), f32),
        ),
        in_specs=[
            pl.BlockSpec(memory_space=pltpu.SMEM),
            pl.BlockSpec(memory_space=pl.ANY),
            vmem, vmem, vmem, vmem,
        ],
        out_specs=(vmem, vmem),
        scratch_shapes=[
            pltpu.VMEM((slots, size, size), bf16),
            pltpu.VMEM((columns, size, rows * capacity * size), bf16),
            pltpu.VMEM((TERMS, rows, length, scenarios), bf16),
            pltpu.VMEM((TERMS, columns, quarter * scenarios, size), bf16),
            pltpu.VMEM((rows, length, scenarios), bf16),
            pltpu.VMEM((columns, quarter * scenarios, size), bf16),
            pltpu.VMEM((4 * capacity * size, quarter * scenarios), bf16),
            pltpu.VMEM((columns * capacity, quarter * scenarios, size), bf16),
            pltpu.VMEM((quarter * scenarios, size), f32),
            pltpu.VMEM((length, scenarios), f32),
            pltpu.VMEM((slabs,) + packed, i16),
            pltpu.VMEM((slabs,) + packed, i16),
            pltpu.VMEM((columns,) + packed, i16),
            pltpu.VMEM((TERMS, slabs) + packed, i16),
            pltpu.VMEM((TERMS, slabs) + packed, i16),
            pltpu.VMEM((TERMS, columns) + packed, i16),
            dma((1,)), dma((slots,)),
            dma((TERMS, slabs)), dma((TERMS, slabs)), dma((TERMS, slabs)), dma((TERMS, slabs)),
            dma((TERMS, columns)), dma((TERMS, columns)),
            dma((TERMS, slabs)), dma((TERMS, slabs)), dma((TERMS, slabs)), dma((TERMS, slabs)),
            dma((TERMS, columns)), dma((TERMS, columns)),
        ],
        compiler_params=pltpu.CompilerParams(
            collective_id=0, has_side_effects=True, vmem_limit_bytes=60 * 2**20
        ),
        name="series",
    )(
        places,
        tiles.reshape(slots, size, size),
        demand,
        value_added,
        extracted.reshape(1, scenarios),
        extracted.reshape(scenarios, 1),
    )


def solution(mesh):
    placed = (
        P("row", "col", None, None, None),
        P(),
        P(("row", "col"), None),
        P(("row", "col"), None),
        P(),
    )
    return jax.shard_map(
        shards,
        mesh=mesh,
        in_specs=placed,
        out_specs=(P(("row", "col"), None), P(("row", "col"), None)),
        check_vma=False,
    )
```

```python
import functools

import jax
import jax.numpy as jnp
from jax import lax
from jax.experimental import pallas as pl
from jax.experimental.pallas import tpu as pltpu
from jax.sharding import PartitionSpec as P

TERMS = 3
GROUPS = 128
LEVEL = 32000.0
MESH = pl.DeviceIdType.MESH


def pack(values, slot):
    rows = values.shape[0]
    top = jnp.max(jnp.abs(values), axis=0, keepdims=True)
    power = jnp.ceil(jnp.log2(jnp.maximum(top, 1e-30)))
    scaled = jnp.floor(values * (jnp.exp2(-power) * LEVEL) + 0.5)
    slot[pl.ds(0, rows), :] = scaled.astype(jnp.int32).astype(jnp.int16)
    slot[pl.ds(rows, 16), :] = (
        jnp.broadcast_to(power, (16, power.shape[1])).astype(jnp.int32).astype(jnp.int16)
    )


def unpack(slot, rows):
    power = slot[pl.ds(rows, 16), :].astype(jnp.int32).astype(jnp.float32)[0:1, :]
    values = slot[pl.ds(0, rows), :].astype(jnp.int32).astype(jnp.float32)
    return values * (jnp.exp2(power) * (1.0 / LEVEL))


def kernel(
    rows, columns, capacity, quarter, places, tiles, demand, value_added, gone,
    quantity, price_out,
    stack, wide, gath_q, gath_p, here_q, here_p, spread_q, spread_p, price, total, keep_down,
    send_x, send_z, send_q, got_x, got_z, got_q,
    tile_sem, out_sem, up_s, down_s, over_r, aqx_s, aqx_r, ap_s, ap_r, px_s, px_r, pz_s, pz_r, q_s, q_r,
):
    size = tiles.shape[1]
    scenarios = demand.shape[1]
    length = quarter * size
    slabs = rows // 2
    group = columns * capacity
    row, column = lax.axis_index("row"), lax.axis_index("col")
    slab, side = row // 2, row % 2
    partner = (slab * 2 + 1 - side, column)

    last = slabs - 1

    def column_peer(step):
        return lax.rem(column + step, columns)

    def remote(src, dst, send, recv, device):
        return pltpu.make_async_remote_copy(
            src_ref=src, dst_ref=dst, send_sem=send, recv_sem=recv,
            device_id=device, device_id_type=MESH,
        )

    whole = pltpu.make_async_copy(tiles, stack, tile_sem.at[0])
    whole.start()

    def side_by_side(m):
        d, u = m // capacity, m % capacity
        place = pl.multiple_of(((d // columns) * capacity + u) * size, size)
        return pltpu.make_async_copy(
            tiles.at[m], wide.at[d % columns, :, pl.ds(place, size)], out_sem.at[m]
        )

    lax.fori_loop(0, rows * group, lambda m, _: (side_by_side(m).start(), 0)[1], 0)

    barrier = pltpu.get_barrier_semaphore()

    def greet(device):
        pl.semaphore_signal(barrier, inc=1, device_id=device, device_id_type=MESH)

    greet(partner)
    pl.when(slab > 0)(lambda: greet((row - 2, column)))
    pl.when(slab < last)(lambda: greet((row + 2, column)))
    for step in range(1, columns):
        greet((row, column_peer(step)))

    first = (row * columns + column) * quarter
    for q in range(quarter):
        part = pl.ds(q * size, size)
        block = (first + q) % GROUPS
        keep = jnp.where(gone[...] != block, 1.0, 0.0)
        start = keep * demand[part, :].astype(jnp.float32)
        quantity[part, :] = start
        gath_q[0, row, part, :] = start.astype(jnp.bfloat16)
        part = pl.ds(q * scenarios, scenarios)
        down = jnp.broadcast_to(keep, (size, scenarios)).T
        keep_down[part, :] = down
        start = down * value_added[pl.ds(q * size, size), :].astype(jnp.float32).T
        price[part, :] = start
        gath_p[0, column, part, :] = start.astype(jnp.bfloat16)

    def move_up(t, z):
        at = gath_q.at[t, z * 2 + side]
        return remote(at, at, up_s.at[t, z], over_r.at[t, z], (row + 2, column))

    def move_down(t, z):
        at = gath_q.at[t, z * 2 + side]
        return remote(at, at, down_s.at[t, z], over_r.at[t, z], (row - 2, column))

    def move_across(t, z):
        at = gath_q.at[t, z * 2 + side]
        return remote(at, at, aqx_s.at[t, z], aqx_r.at[t, z], partner)

    def move_from_across(t, z):
        at = gath_q.at[t, z * 2 + 1 - side]
        return remote(at, at, aqx_s.at[t, z], aqx_r.at[t, z], partner)

    def charge_to(t, step):
        at = gath_p.at[t, column]
        return remote(at, at, ap_s.at[t, step], ap_r.at[t, column], (row, column_peer(step)))

    def charge_from(t, c):
        at = gath_p.at[t, c]
        return remote(at, at, ap_s.at[t, 0], ap_r.at[t, c], partner)

    def cost_across(t, z):
        return remote(send_x.at[z], got_x.at[t, z], px_s.at[t, z], px_r.at[t, z], partner)

    def cost_up(t, z):
        return remote(
            send_z.at[z], got_z.at[t, z], pz_s.at[t, z], pz_r.at[t, z], (row + 2, column)
        )

    def cost_down(t, z):
        slot = jnp.where(z == slab - 1, slabs, z)
        return remote(
            send_z.at[z], got_z.at[t, slot], pz_s.at[t, z], pz_r.at[t, slot], (row - 2, column)
        )

    def cost_in(t, slot):
        return remote(send_z.at[0], got_z.at[t, slot], pz_s.at[t, 0], pz_r.at[t, slot], partner)

    def image_to(t, step):
        return remote(
            send_q.at[step], got_q.at[t, column], q_s.at[t, step], q_r.at[t, column],
            (row, column_peer(step)),
        )

    def image_from(t, c):
        return remote(send_q.at[0], got_q.at[t, c], q_s.at[t, 0], q_r.at[t, c], partner)

    def each(low, high, body):
        lax.fori_loop(low, high, lambda i, _: (body(i), 0)[1], 0)

    def send_charge(t):
        each(1, columns, lambda s: charge_to(t, s).start())

    def send_move(t):
        pl.when(slab < last)(lambda: move_up(t, slab).start())
        pl.when(slab > 0)(lambda: move_down(t, slab).start())
        move_across(t, slab).start()

    ends = jnp.where(slab > 0, 1, 0) + jnp.where(slab < last, 1, 0)
    pl.semaphore_wait(barrier, columns + ends)
    send_charge(0)
    send_move(0)
    whole.wait()
    lax.fori_loop(0, rows * group, lambda m, _: (side_by_side(m).wait(), 0)[1], 0)

    def weight(ok):
        return jnp.full((16, 128), jnp.where(ok, 1.0, 0.0), jnp.float32).astype(jnp.bfloat16)

    def charge_part(owner):
        def fill(k, _):
            place = places[row, column, owner * group + k]
            at = (k // capacity) * quarter + place // quarter
            block = here_p[at // quarter, pl.ds((at % quarter) * scenarios, scenarios), :]
            block = block.reshape(scenarios // 16, 16, size)
            for q in range(quarter):
                spread_p[k, pl.ds(q * scenarios, scenarios), :] = (
                    block * weight(place % quarter == q)[None]
                ).reshape(scenarios, size)
            return 0

        lax.fori_loop(0, group, fill, 0, unroll=True)
        left = jnp.concatenate([spread_p[k] for k in range(group)], axis=1)
        right = stack[pl.ds(owner * group, group)].reshape(group * size, size)
        return jnp.dot(left, right, preferred_element_type=jnp.float32)

    def supply_part(owner):
        width = 4

        def chunk(j, _):
            for k in range(width * capacity):
                source = j * width + k // capacity
                place = places[row, column, (source * columns + owner) * capacity + k % capacity]
                block = here_q[source, pl.ds((place % quarter) * size, size), :]
                block = block.reshape(size // 16, 16, scenarios)
                for q in range(quarter):
                    spread_q[pl.ds(k * size, size), pl.ds(q * scenarios, scenarios)] = (
                        block * weight(place // quarter == q)[None]
                    ).reshape(size, scenarios)
            depth = width * capacity * size
            left = wide[owner, :, pl.ds(pl.multiple_of(j * depth, depth), depth)]
            product = jnp.dot(left, spread_q[...], preferred_element_type=jnp.float32)
            for q in range(quarter):
                part = product[:, q * scenarios : (q + 1) * scenarios]
                total[pl.ds(q * size, size), :] += part
            return 0

        total[...] = jnp.zeros_like(total)
        lax.fori_loop(0, rows // width, chunk, 0)

    def owner_slab(j):
        falling = jnp.where(last - j > slab, last - j, last - j - 1)
        rising = jnp.where(j < slab, j, j + 1)
        other = jnp.where(slab < slabs // 2, falling, rising)
        return jnp.where(j == last, slab, other)

    def term(t, _):
        def pass_on(s):
            @pl.when(slab >= s)
            def _():
                z = slab - s
                move_down(t, z).wait_recv()
                pl.when(slab < last)(lambda: move_up(t, z).start())
                move_across(t, z).start()

            @pl.when(slab + s <= last)
            def _():
                z = slab + s
                move_down(t, z).wait_recv()
                pl.when(slab > 0)(lambda: move_down(t, z).start())
                move_across(t, z).start()

        def give_across(j):
            z = owner_slab(j)
            pack(charge_part(z * 2 + 1 - side), send_x.at[z])
            cost_across(t, z).start()

        def give_on(j):
            z = owner_slab(j)
            total[...] = charge_part(z * 2 + side)
            cost_across(t, z).wait_recv()
            total[...] += unpack(got_x.at[t, z], length)

            @pl.when(jnp.where(z > slab, slab > 0, slab < last))
            def _():
                cost_in(t, z).wait_recv()
                total[...] += unpack(got_z.at[t, z], length)

            pack(total[...], send_z.at[z])
            pl.when(z > slab)(lambda: cost_up(t, z).start())
            pl.when(z < slab)(lambda: cost_down(t, z).start())

        def give_image(s):
            supply_part(column_peer(s))
            pack(total[...], send_q.at[s])
            image_to(t, s).start()

        pass_on(1)
        each(1, columns, lambda s: charge_from(t, column_peer(s)).wait_recv())
        here_p[...] = gath_p[t]

        def both(j):
            give_across(j)
            pass_on(j + 2)

        each(0, slabs - 2, both)
        each(slabs - 2, slabs, give_across)
        give_on(0)
        each(0, slabs, lambda z: move_from_across(t, z).wait_recv())

        def bring(i):
            here_q[i] = gath_q[t, i]

        each(0, rows, bring)
        each(1, columns, give_image)
        each(1, last, give_on)

        supply_part(column)
        image = total[...]
        for s in range(1, columns):
            c = column_peer(s)
            image_from(t, c).wait_recv()
            image += unpack(got_q.at[t, c], length)
        for q in range(quarter):
            part = pl.ds(q * size, size)
            keep = jnp.where(gone[...] != (first + q) % GROUPS, 1.0, 0.0)
            masked = keep * image[q * size : (q + 1) * size]
            quantity[part, :] += masked
            gath_q[lax.rem(t + 1, TERMS), row, part, :] = masked.astype(jnp.bfloat16)
        pl.when(t + 1 < TERMS)(lambda: send_move(t + 1))

        total[...] = charge_part(row)
        cost_across(t, slab).wait_recv()
        total[...] += unpack(got_x.at[t, slab], length)

        @pl.when(slab > 0)
        def _():
            cost_in(t, slab).wait_recv()
            total[...] += unpack(got_z.at[t, slab], length)

        @pl.when(slab < last)
        def _():
            cost_in(t, slabs).wait_recv()
            total[...] += unpack(got_z.at[t, slabs], length)

        masked = keep_down[...] * total[...]
        price[...] += masked
        gath_p[lax.rem(t + 1, TERMS), column] = masked.astype(jnp.bfloat16)
        pl.when(t + 1 < TERMS)(lambda: send_charge(t + 1))

        each(1, columns, lambda s: charge_to(t, s).wait_send())
        each(1, columns, lambda s: image_to(t, s).wait_send())
        each(0, slabs, lambda z: move_across(t, z).wait_send())
        each(0, slabs, lambda z: cost_across(t, z).wait_send())
        pl.when(slab < last)(lambda: each(0, slab + 1, lambda z: move_up(t, z).wait_send()))
        pl.when(slab > 0)(lambda: each(slab, slabs, lambda z: move_down(t, z).wait_send()))
        each(0, last, lambda j: cost_up(t, owner_slab(j)).wait_send())
        return 0

    lax.fori_loop(0, TERMS, term, 0)
    for q in range(quarter):
        price_out[pl.ds(q * size, size), :] = price[pl.ds(q * scenarios, scenarios), :].T


def shards(tiles, positions, demand, value_added, extracted):
    rows, columns = lax.axis_size("row"), lax.axis_size("col")
    slots, size = tiles.shape[2], tiles.shape[-1]
    length, scenarios = demand.shape
    quarter = length // size
    capacity = slots // (rows * columns)
    slabs = rows // 2
    dma = pltpu.SemaphoreType.DMA
    vmem = pl.BlockSpec(memory_space=pltpu.VMEM)
    bf16, f32, i16 = jnp.bfloat16, jnp.float32, jnp.int16
    packed = (length + 16, scenarios)
    return pl.pallas_call(
        functools.partial(kernel, rows, columns, capacity, quarter),
        out_shape=(
            jax.ShapeDtypeStruct((length, scenarios), f32),
            jax.ShapeDtypeStruct((length, scenarios), f32),
        ),
        in_specs=[
            pl.BlockSpec(memory_space=pltpu.SMEM),
            pl.BlockSpec(memory_space=pl.ANY),
            vmem, vmem, vmem,
        ],
        out_specs=(vmem, vmem),
        scratch_shapes=[
            pltpu.VMEM((slots, size, size), bf16),
            pltpu.VMEM((columns, size, rows * capacity * size), bf16),
            pltpu.VMEM((TERMS, rows, length, scenarios), bf16),
            pltpu.VMEM((TERMS, columns, quarter * scenarios, size), bf16),
            pltpu.VMEM((rows, length, scenarios), bf16),
            pltpu.VMEM((columns, quarter * scenarios, size), bf16),
            pltpu.VMEM((4 * capacity * size, quarter * scenarios), bf16),
            pltpu.VMEM((columns * capacity, quarter * scenarios, size), bf16),
            pltpu.VMEM((quarter * scenarios, size), f32),
            pltpu.VMEM((length, scenarios), f32),
            pltpu.VMEM((quarter * scenarios, size), f32),
            pltpu.VMEM((slabs,) + packed, i16),
            pltpu.VMEM((slabs,) + packed, i16),
            pltpu.VMEM((columns,) + packed, i16),
            pltpu.VMEM((TERMS, slabs) + packed, i16),
            pltpu.VMEM((TERMS, slabs + 1) + packed, i16),
            pltpu.VMEM((TERMS, columns) + packed, i16),
            dma((1,)), dma((slots,)),
            dma((TERMS, slabs)), dma((TERMS, slabs)), dma((TERMS, slabs)),
            dma((TERMS, slabs)), dma((TERMS, slabs)),
            dma((TERMS, columns)), dma((TERMS, columns)),
            dma((TERMS, slabs)), dma((TERMS, slabs)),
            dma((TERMS, slabs)), dma((TERMS, slabs + 1)),
            dma((TERMS, columns)), dma((TERMS, columns)),
        ],
        compiler_params=pltpu.CompilerParams(
            collective_id=0, has_side_effects=True, vmem_limit_bytes=61 * 2**20
        ),
        name="series",
    )(
        positions,
        tiles.reshape(slots, size, size),
        demand,
        value_added,
        extracted.reshape(1, scenarios),
    )


def solution(mesh):
    placed = (
        P("row", "col", None, None, None),
        P(),
        P(("row", "col"), None),
        P(("row", "col"), None),
        P(),
    )
    return jax.shard_map(
        shards,
        mesh=mesh,
        in_specs=placed,
        out_specs=(P(("row", "col"), None), P(("row", "col"), None)),
        check_vma=False,
    )
```

```python
import functools

import jax
import jax.numpy as jnp
from jax import lax
from jax.experimental import pallas as pl
from jax.experimental.pallas import tpu as pltpu
from jax.sharding import PartitionSpec as P

TERMS = 3
GROUPS = 128
LEVEL = 32000.0
MESH = pl.DeviceIdType.MESH


def pack(values, slot):
    rows = values.shape[0]
    top = jnp.max(jnp.abs(values), axis=0, keepdims=True)
    power = jnp.ceil(jnp.log2(jnp.maximum(top, 1e-30)))
    scaled = jnp.floor(values * (jnp.exp2(-power) * LEVEL) + 0.5)
    slot[pl.ds(0, rows), :] = scaled.astype(jnp.int32).astype(jnp.int16)
    slot[pl.ds(rows, 16), :] = (
        jnp.broadcast_to(power, (16, power.shape[1])).astype(jnp.int32).astype(jnp.int16)
    )


def unpack(slot, rows):
    power = slot[pl.ds(rows, 16), :].astype(jnp.int32).astype(jnp.float32)[0:1, :]
    values = slot[pl.ds(0, rows), :].astype(jnp.int32).astype(jnp.float32)
    return values * (jnp.exp2(power) * (1.0 / LEVEL))


def kernel(
    rows, columns, capacity, quarter, places, tiles, demand, value_added, gone,
    quantity, price_out,
    stack, wide, gath_q, gath_p, here_q, here_p, spread_q, spread_p, price, total, keep_down,
    send_x, send_z, send_q, got_x, got_z, got_q,
    tile_sem, out_sem, up_s, down_s, over_r, aqx_s, aqx_r, ap_s, ap_r, px_s, px_r, pz_s, pz_r, q_s, q_r,
):
    size = tiles.shape[1]
    scenarios = demand.shape[1]
    length = quarter * size
    slabs = rows // 2
    group = columns * capacity
    row, column = lax.axis_index("row"), lax.axis_index("col")
    slab, side = row // 2, row % 2
    partner = (slab * 2 + 1 - side, column)

    last = slabs - 1

    def column_peer(step):
        return lax.rem(column + step, columns)

    def remote(src, dst, send, recv, device):
        return pltpu.make_async_remote_copy(
            src_ref=src, dst_ref=dst, send_sem=send, recv_sem=recv,
            device_id=device, device_id_type=MESH,
        )

    whole = pltpu.make_async_copy(tiles, stack, tile_sem.at[0])
    whole.start()

    def side_by_side(m):
        d, u = m // capacity, m % capacity
        place = pl.multiple_of(((d // columns) * capacity + u) * size, size)
        return pltpu.make_async_copy(
            tiles.at[m], wide.at[d % columns, :, pl.ds(place, size)], out_sem.at[m]
        )

    lax.fori_loop(0, rows * group, lambda m, _: (side_by_side(m).start(), 0)[1], 0)

    barrier = pltpu.get_barrier_semaphore()

    def greet(device):
        pl.semaphore_signal(barrier, inc=1, device_id=device, device_id_type=MESH)

    greet(partner)
    pl.when(slab > 0)(lambda: greet((row - 2, column)))
    pl.when(slab < last)(lambda: greet((row + 2, column)))
    for step in range(1, columns):
        greet((row, column_peer(step)))

    first = (row * columns + column) * quarter
    for q in range(quarter):
        part = pl.ds(q * size, size)
        block = (first + q) % GROUPS
        keep = jnp.where(gone[...] != block, 1.0, 0.0)
        start = keep * demand[part, :].astype(jnp.float32)
        quantity[part, :] = start
        gath_q[0, row, part, :] = start.astype(jnp.bfloat16)
        part = pl.ds(q * scenarios, scenarios)
        down = jnp.broadcast_to(keep, (size, scenarios)).T
        keep_down[part, :] = down
        start = down * value_added[pl.ds(q * size, size), :].astype(jnp.float32).T
        price[part, :] = start
        gath_p[0, column, part, :] = start.astype(jnp.bfloat16)

    def move_up(t, z):
        at = gath_q.at[t, z * 2 + side]
        return remote(at, at, up_s.at[t, z], over_r.at[t, z], (row + 2, column))

    def move_down(t, z):
        at = gath_q.at[t, z * 2 + side]
        return remote(at, at, down_s.at[t, z], over_r.at[t, z], (row - 2, column))

    def move_across(t, z):
        at = gath_q.at[t, z * 2 + side]
        return remote(at, at, aqx_s.at[t, z], aqx_r.at[t, z], partner)

    def move_from_across(t, z):
        at = gath_q.at[t, z * 2 + 1 - side]
        return remote(at, at, aqx_s.at[t, z], aqx_r.at[t, z], partner)

    def charge_to(t, step):
        at = gath_p.at[t, column]
        return remote(at, at, ap_s.at[t, step], ap_r.at[t, column], (row, column_peer(step)))

    def charge_from(t, c):
        at = gath_p.at[t, c]
        return remote(at, at, ap_s.at[t, 0], ap_r.at[t, c], partner)

    def cost_across(t, z):
        return remote(send_x.at[z], got_x.at[t, z], px_s.at[t, z], px_r.at[t, z], partner)

    def cost_up(t, z):
        return remote(
            send_z.at[z], got_z.at[t, z], pz_s.at[t, z], pz_r.at[t, z], (row + 2, column)
        )

    def cost_down(t, z):
        slot = jnp.where(z == slab - 1, slabs, z)
        return remote(
            send_z.at[z], got_z.at[t, slot], pz_s.at[t, z], pz_r.at[t, slot], (row - 2, column)
        )

    def cost_in(t, slot):
        return remote(send_z.at[0], got_z.at[t, slot], pz_s.at[t, 0], pz_r.at[t, slot], partner)

    def image_to(t, step):
        return remote(
            send_q.at[step], got_q.at[t, column], q_s.at[t, step], q_r.at[t, column],
            (row, column_peer(step)),
        )

    def image_from(t, c):
        return remote(send_q.at[0], got_q.at[t, c], q_s.at[t, 0], q_r.at[t, c], partner)

    def each(low, high, body):
        lax.fori_loop(low, high, lambda i, _: (body(i), 0)[1], 0)

    def send_charge(t):
        each(1, columns, lambda s: charge_to(t, s).start())

    def send_move(t):
        pl.when(slab < last)(lambda: move_up(t, slab).start())
        pl.when(slab > 0)(lambda: move_down(t, slab).start())
        move_across(t, slab).start()

    ends = jnp.where(slab > 0, 1, 0) + jnp.where(slab < last, 1, 0)
    pl.semaphore_wait(barrier, columns + ends)
    send_charge(0)
    send_move(0)
    whole.wait()
    lax.fori_loop(0, rows * group, lambda m, _: (side_by_side(m).wait(), 0)[1], 0)

    def weight(ok):
        return jnp.full((16, 128), jnp.where(ok, 1.0, 0.0), jnp.float32).astype(jnp.bfloat16)

    def charge_part(owner):
        def fill(k, _):
            place = places[row, column, owner * group + k]
            at = (k // capacity) * quarter + place // quarter
            block = here_p[at // quarter, pl.ds((at % quarter) * scenarios, scenarios), :]
            block = block.reshape(scenarios // 16, 16, size)
            for q in range(quarter):
                spread_p[k, pl.ds(q * scenarios, scenarios), :] = (
                    block * weight(place % quarter == q)[None]
                ).reshape(scenarios, size)
            return 0

        lax.fori_loop(0, group, fill, 0, unroll=True)
        left = jnp.concatenate([spread_p[k] for k in range(group)], axis=1)
        right = stack[pl.ds(owner * group, group)].reshape(group * size, size)
        return jnp.dot(left, right, preferred_element_type=jnp.float32)

    def supply_part(owner):
        width = 4

        def chunk(j, _):
            for k in range(width * capacity):
                source = j * width + k // capacity
                place = places[row, column, (source * columns + owner) * capacity + k % capacity]
                block = here_q[source, pl.ds((place % quarter) * size, size), :]
                block = block.reshape(size // 16, 16, scenarios)
                for q in range(quarter):
                    spread_q[pl.ds(k * size, size), pl.ds(q * scenarios, scenarios)] = (
                        block * weight(place // quarter == q)[None]
                    ).reshape(size, scenarios)
            depth = width * capacity * size
            left = wide[owner, :, pl.ds(pl.multiple_of(j * depth, depth), depth)]
            product = jnp.dot(left, spread_q[...], preferred_element_type=jnp.float32)
            for q in range(quarter):
                part = product[:, q * scenarios : (q + 1) * scenarios]
                total[pl.ds(q * size, size), :] += part
            return 0

        total[...] = jnp.zeros_like(total)
        lax.fori_loop(0, rows // width, chunk, 0)

    def owner_slab(j):
        falling = jnp.where(last - j > slab, last - j, last - j - 1)
        rising = jnp.where(j < slab, j, j + 1)
        other = jnp.where(slab < slabs // 2, falling, rising)
        return jnp.where(j == last, slab, other)

    def term(t, _):
        def pass_on(s):
            @pl.when(slab >= s)
            def _():
                z = slab - s
                move_down(t, z).wait_recv()
                pl.when(slab < last)(lambda: move_up(t, z).start())
                move_across(t, z).start()

            @pl.when(slab + s <= last)
            def _():
                z = slab + s
                move_down(t, z).wait_recv()
                pl.when(slab > 0)(lambda: move_down(t, z).start())
                move_across(t, z).start()

        def give_across(j):
            z = owner_slab(j)
            pack(charge_part(z * 2 + 1 - side), send_x.at[z])
            cost_across(t, z).start()

        def give_on(j):
            z = owner_slab(j)
            total[...] = charge_part(z * 2 + side)
            cost_across(t, z).wait_recv()
            total[...] += unpack(got_x.at[t, z], length)

            @pl.when(jnp.where(z > slab, slab > 0, slab < last))
            def _():
                cost_in(t, z).wait_recv()
                total[...] += unpack(got_z.at[t, z], length)

            pack(total[...], send_z.at[z])
            pl.when(z > slab)(lambda: cost_up(t, z).start())
            pl.when(z < slab)(lambda: cost_down(t, z).start())

        def give_image(s):
            supply_part(column_peer(s))
            pack(total[...], send_q.at[s])
            image_to(t, s).start()

        pass_on(1)
        each(1, columns, lambda s: charge_from(t, column_peer(s)).wait_recv())
        here_p[...] = gath_p[t]

        def both(j):
            give_across(j)
            pass_on(j + 2)

        each(0, slabs - 2, both)
        each(slabs - 2, slabs, give_across)
        each(0, last, give_on)
        each(0, slabs, lambda z: move_from_across(t, z).wait_recv())

        def bring(i):
            here_q[i] = gath_q[t, i]

        each(0, rows, bring)
        each(1, columns, give_image)

        supply_part(column)
        image = total[...]
        for s in range(1, columns):
            c = column_peer(s)
            image_from(t, c).wait_recv()
            image += unpack(got_q.at[t, c], length)
        for q in range(quarter):
            part = pl.ds(q * size, size)
            keep = jnp.where(gone[...] != (first + q) % GROUPS, 1.0, 0.0)
            masked = keep * image[q * size : (q + 1) * size]
            quantity[part, :] += masked
            gath_q[lax.rem(t + 1, TERMS), row, part, :] = masked.astype(jnp.bfloat16)
        pl.when(t + 1 < TERMS)(lambda: send_move(t + 1))

        total[...] = charge_part(row)
        cost_across(t, slab).wait_recv()
        total[...] += unpack(got_x.at[t, slab], length)

        @pl.when(slab > 0)
        def _():
            cost_in(t, slab).wait_recv()
            total[...] += unpack(got_z.at[t, slab], length)

        @pl.when(slab < last)
        def _():
            cost_in(t, slabs).wait_recv()
            total[...] += unpack(got_z.at[t, slabs], length)

        masked = keep_down[...] * total[...]
        price[...] += masked
        gath_p[lax.rem(t + 1, TERMS), column] = masked.astype(jnp.bfloat16)
        pl.when(t + 1 < TERMS)(lambda: send_charge(t + 1))

        each(1, columns, lambda s: charge_to(t, s).wait_send())
        each(1, columns, lambda s: image_to(t, s).wait_send())
        each(0, slabs, lambda z: move_across(t, z).wait_send())
        each(0, slabs, lambda z: cost_across(t, z).wait_send())
        pl.when(slab < last)(lambda: each(0, slab + 1, lambda z: move_up(t, z).wait_send()))
        pl.when(slab > 0)(lambda: each(slab, slabs, lambda z: move_down(t, z).wait_send()))
        each(0, last, lambda j: cost_up(t, owner_slab(j)).wait_send())
        return 0

    lax.fori_loop(0, TERMS, term, 0)
    for q in range(quarter):
        price_out[pl.ds(q * size, size), :] = price[pl.ds(q * scenarios, scenarios), :].T


def shards(tiles, positions, demand, value_added, extracted):
    rows, columns = lax.axis_size("row"), lax.axis_size("col")
    slots, size = tiles.shape[2], tiles.shape[-1]
    length, scenarios = demand.shape
    quarter = length // size
    capacity = slots // (rows * columns)
    slabs = rows // 2
    dma = pltpu.SemaphoreType.DMA
    vmem = pl.BlockSpec(memory_space=pltpu.VMEM)
    bf16, f32, i16 = jnp.bfloat16, jnp.float32, jnp.int16
    packed = (length + 16, scenarios)
    return pl.pallas_call(
        functools.partial(kernel, rows, columns, capacity, quarter),
        out_shape=(
            jax.ShapeDtypeStruct((length, scenarios), f32),
            jax.ShapeDtypeStruct((length, scenarios), f32),
        ),
        in_specs=[
            pl.BlockSpec(memory_space=pltpu.SMEM),
            pl.BlockSpec(memory_space=pl.ANY),
            vmem, vmem, vmem,
        ],
        out_specs=(vmem, vmem),
        scratch_shapes=[
            pltpu.VMEM((slots, size, size), bf16),
            pltpu.VMEM((columns, size, rows * capacity * size), bf16),
            pltpu.VMEM((TERMS, rows, length, scenarios), bf16),
            pltpu.VMEM((TERMS, columns, quarter * scenarios, size), bf16),
            pltpu.VMEM((rows, length, scenarios), bf16),
            pltpu.VMEM((columns, quarter * scenarios, size), bf16),
            pltpu.VMEM((4 * capacity * size, quarter * scenarios), bf16),
            pltpu.VMEM((columns * capacity, quarter * scenarios, size), bf16),
            pltpu.VMEM((quarter * scenarios, size), f32),
            pltpu.VMEM((length, scenarios), f32),
            pltpu.VMEM((quarter * scenarios, size), f32),
            pltpu.VMEM((slabs,) + packed, i16),
            pltpu.VMEM((slabs,) + packed, i16),
            pltpu.VMEM((columns,) + packed, i16),
            pltpu.VMEM((TERMS, slabs) + packed, i16),
            pltpu.VMEM((TERMS, slabs + 1) + packed, i16),
            pltpu.VMEM((TERMS, columns) + packed, i16),
            dma((1,)), dma((slots,)),
            dma((TERMS, slabs)), dma((TERMS, slabs)), dma((TERMS, slabs)),
            dma((TERMS, slabs)), dma((TERMS, slabs)),
            dma((TERMS, columns)), dma((TERMS, columns)),
            dma((TERMS, slabs)), dma((TERMS, slabs)),
            dma((TERMS, slabs)), dma((TERMS, slabs + 1)),
            dma((TERMS, columns)), dma((TERMS, columns)),
        ],
        compiler_params=pltpu.CompilerParams(
            collective_id=0, has_side_effects=True, vmem_limit_bytes=61 * 2**20
        ),
        name="series",
    )(
        positions,
        tiles.reshape(slots, size, size),
        demand,
        value_added,
        extracted.reshape(1, scenarios),
    )


def solution(mesh):
    placed = (
        P("row", "col", None, None, None),
        P(),
        P(("row", "col"), None),
        P(("row", "col"), None),
        P(),
    )
    return jax.shard_map(
        shards,
        mesh=mesh,
        in_specs=placed,
        out_specs=(P(("row", "col"), None), P(("row", "col"), None)),
        check_vma=False,
    )
```
